32 devices in a mesh: ty: 4 (over z), tx: 8 (over y, x, core).
Axes of the slice: x: 2, y: 2, z: 4, core: 2. Of those that a mesh axis runs over, the one named last changes fastest.
Arguments:
- specimen: float32 [2, 4096, 4096], P(None, 'ty', 'tx'), may hold values from -6 to 6
- probe_modes: float32 [2, 3, 512, 512], replicated, may hold values from -6 to 6
- amplitude: float32 [64, 512, 512], P(('ty', 'tx')), may hold values from 0.5 to 3
- offsets: int32 [64, 2], P(('ty', 'tx')), may hold values from 0 to 1023, as said below
- live_slots: int32 [64], P(('ty', 'tx')), may hold values from 0 to 1, as said below
Outputs:
- specimen_grad: float32 [2, 4096, 4096], P(None, 'ty', 'tx')
- probe_grad: float32 [2, 3, 512, 512], replicated
The draws below stay inside these ranges and needn't reach their ends.
Inputs may be any that keep to these rules, and one draw needn't show every extreme that they name: `offsets`: offsets are a row below 1024 and a column below 512 within the tile of the slot's device, chosen so that the 512 x 512 patch lies inside the object. `live_slots`: on each device the live slots come first; the two devices with tx indices 2m and 2m+1 and the same ty index hold exactly 2 live slots together.
All inputs are finite; a program needn't handle non-finite values.
Results may differ from the reference program's by a relative error of at most 0.0038.
The reference program's roundings to bfloat16 on the way count: a program that leaves them out, or rounds other values in their place, can miss the bound.
Values sent between devices are 32-bit elements; how exact they have to be, the bound alone decides.
A program may use at most 128 MiB of HBM per device.

```python
import math
import jax
import jax.numpy as jnp
from jax import lax

PATCH = 512
MODES = 3
TH = 1024
TW = 512
CAP = 2
OBJ_H = 4096
OBJ_W = 4096
SLOTS = 64
N_TX = 8


def draw_live_slots(key, part):
    devices_all = SLOTS // CAP
    first_count = jax.random.randint(key, (devices_all,), 1, CAP + 1)
    device = jnp.arange(devices_all, dtype=jnp.int32)
    pair_first = device - device % 2
    leader = jnp.where(pair_first == 0, 1, first_count[pair_first])
    leader = jnp.where(pair_first == devices_all - 2, 0, leader)
    holding = jnp.where(device % 2 == 0, leader, CAP - leader)
    slot_index = jnp.arange(SLOTS, dtype=jnp.int32)
    return (slot_index % CAP < holding[slot_index // CAP]).astype(jnp.int32)


def draw_offsets(key, part):
    tile_rows = OBJ_H // TH
    tile_cols = OBJ_W // TW
    slot_index = jnp.arange(SLOTS, dtype=jnp.int32)
    device = slot_index // CAP
    row_limit = jnp.where(device // tile_cols == tile_rows - 1, TH - PATCH + 1, TH)
    col_limit = jnp.where(device % tile_cols == tile_cols - 1, TW - PATCH + 1, TW)
    key_rows = jax.random.fold_in(key, 11)
    key_cols = jax.random.fold_in(key, 23)
    row_at = jax.random.randint(key_rows, (SLOTS,), 0, row_limit)
    col_at = jax.random.randint(key_cols, (SLOTS,), 0, col_limit)
    first_slot = slot_index % CAP == 0
    row_at = jnp.where(first_slot, row_limit - 1, row_at)
    col_at = jnp.where(first_slot, col_limit - 1, col_at)
    return jnp.stack([row_at, col_at], axis=1).astype(jnp.int32)


def shard_levels(rng, shape, pieces, least, top_value):
    factor_of = 1.0
    for axis_at, shards_of in pieces:
        draws = jax.random.uniform(jax.random.fold_in(jax.random.fold_in(rng, 6), axis_at), (shards_of,), jnp.float32, least / len(pieces), top_value / len(pieces))
        factor_of = factor_of * jnp.repeat(jnp.exp(draws), shape[axis_at] // shards_of).reshape((-1,) + (1,) * (len(shape) - 1 - axis_at))
    return factor_of


def normal_values(stream_key, extent, scale, limit, pieces=(), kind=jnp.bfloat16):
    level = shard_levels(stream_key, extent, pieces, -0.22, 0.18) if pieces else 1.0
    result = jax.random.normal(stream_key, extent, jnp.float32) * scale * level
    return jnp.minimum(jnp.maximum(result, -limit), limit).astype(kind)


def setup_inputs(seed: int = 0) -> dict:
    key_list = jax.random.split(jax.random.key(seed), 6)
    return {
        "specimen": normal_values(key_list[0], (2, OBJ_H, OBJ_W), 0.7, 6.0, ((1, 4), (2, 8)), jnp.float32),
        "probe_modes": normal_values(key_list[1], (2, MODES, PATCH, PATCH), 0.6, 6.0, (), jnp.float32),
        "amplitude": jnp.clip(jnp.exp(math.log(3.0) - 1.7917595 * jax.random.uniform(key_list[2], (SLOTS, PATCH, PATCH), jnp.float32) ** shard_levels(key_list[2], (SLOTS, PATCH, PATCH), ((0, 32),), -0.2, 0.2)), 0.5, 3.0),
        "offsets": draw_offsets(jax.random.fold_in(key_list[5], 71), 0),
        "live_slots": draw_live_slots(jax.random.fold_in(key_list[5], 71), 0),
    }


def tables(length):
    index = jnp.arange(length, dtype=jnp.int32)
    phase = index[:, None] * index[None, :] % length
    angle = phase.astype(jnp.float32) * (2.0 * math.pi / length)
    scale = 1.0 / math.sqrt(length)
    return ((jnp.cos(angle) * scale).astype(jnp.bfloat16), (jnp.sin(angle) * scale).astype(jnp.bfloat16))

def left_product(matrix, stacked):
    return jnp.einsum('ij,mjk->mik', matrix.astype(jnp.float32), stacked.astype(jnp.float32))

def right_product(stacked, matrix):
    return jnp.einsum('mij,jk->mik', stacked.astype(jnp.float32), matrix.astype(jnp.float32))

def transform(real_part, imag_part, cos_table, sin_table, orient):
    length = real_part.shape[-1]
    stacked = jnp.concatenate([real_part, imag_part], axis=2)
    cos_part = left_product(cos_table, stacked)
    sin_part = left_product(sin_table, stacked)
    middle_re = (cos_part[:, :, :length] + orient * sin_part[:, :, length:]).astype(jnp.bfloat16)
    middle_im = (cos_part[:, :, length:] - orient * sin_part[:, :, :length]).astype(jnp.bfloat16)
    stacked = jnp.concatenate([middle_re, middle_im], axis=1)
    cos_part = right_product(stacked, cos_table)
    sin_part = right_product(stacked, sin_table)
    result_re = cos_part[:, :length] + orient * sin_part[:, length:]
    result_im = cos_part[:, length:] - orient * sin_part[:, :length]
    return (result_re, result_im)

def slot_terms(window, probe_modes, measured, alive_mask, cos_table, sin_table):
    window_re, window_im = (window[0], window[1])
    probe_re, probe_im = (probe_modes[0], probe_modes[1])
    wave_re = (probe_re * window_re - probe_im * window_im).astype(jnp.bfloat16)
    wave_im = (probe_re * window_im + probe_im * window_re).astype(jnp.bfloat16)
    far_re, far_im = transform(wave_re, wave_im, cos_table, sin_table, 1.0)
    intensity = lax.optimization_barrier(jnp.sum(far_re * far_re + far_im * far_im, axis=0))
    factor = measured * lax.rsqrt(jnp.maximum(intensity, 1.0)) - 1.0
    delta_re = (far_re * factor).astype(jnp.bfloat16)
    delta_im = (far_im * factor).astype(jnp.bfloat16)
    back_re, back_im = transform(delta_re, delta_im, cos_table, sin_table, -1.0)
    back_re = back_re * alive_mask
    back_im = back_im * alive_mask
    grad_re = lax.optimization_barrier(jnp.sum(probe_re * back_re + probe_im * back_im, axis=0))
    grad_im = lax.optimization_barrier(jnp.sum(probe_re * back_im - probe_im * back_re, axis=0))
    mode_re = window_re * back_re + window_im * back_im
    mode_im = window_re * back_im - window_im * back_re
    return (jnp.stack([grad_re, grad_im]), jnp.stack([mode_re, mode_im]))

def reference(specimen, probe_modes, amplitude, offsets, live_slots):
    cos_table, sin_table = tables(PATCH)
    alive_all = live_slots.astype(jnp.float32)
    slot_index = jnp.arange(SLOTS, dtype=jnp.int32)
    device = slot_index // CAP
    row_start = (device // N_TX * TH + offsets[:, 0]).astype(jnp.int32)
    col_start = (device % N_TX * TW + offsets[:, 1]).astype(jnp.int32)
    anchor = jnp.zeros((), jnp.int32)

    def visit(carry, slot_items):
        grad_total, probe_total = carry
        row_at, col_at, measured, alive_mask = slot_items
        window = lax.dynamic_slice(specimen, (anchor, row_at, col_at), (2, PATCH, PATCH))
        grad_term, probe_term = slot_terms(window, probe_modes, measured, alive_mask, cos_table, sin_table)
        current = lax.dynamic_slice(grad_total, (anchor, row_at, col_at), (2, PATCH, PATCH))
        grad_total = lax.dynamic_update_slice(grad_total, current + grad_term, (anchor, row_at, col_at))
        return ((grad_total, probe_total + probe_term), None)
    start = (jnp.zeros(specimen.shape, jnp.float32), jnp.zeros(probe_modes.shape, jnp.float32))
    (grad_total, probe_total), _ = lax.scan(visit, start, (row_start, col_start, amplitude, alive_all))
    return (grad_total, probe_total * (1.0 / math.sqrt(SLOTS)))
```

```python
import functools
import math

import jax
import jax.numpy as jnp
import ml_dtypes
import numpy as np
from jax import lax
from jax.experimental import pallas as pl
from jax.experimental.pallas import tpu as pltpu
from jax.sharding import PartitionSpec as P

CHUNKS = 2
ROWS = 32


def flipped(value, axis, bit):
    mask = 1 << bit
    return lax.ppermute(value, axis, [(at, at ^ mask) for at in range(lax.axis_size(axis))])


def shifted(value, axis, steps):
    count = lax.axis_size(axis)
    first, last = max(0, -steps), min(count, count - steps)
    return lax.ppermute(value, axis, [(at, at + steps) for at in range(first, last)])


def block_tables(length):
    index = np.arange(length)
    angle = (index[:, None] * index[None, :] % length) * (2.0 * math.pi / length)
    scale = 1.0 / math.sqrt(length)
    cos = (np.cos(angle) * scale).astype(np.float32)
    sin = (np.sin(angle) * scale).astype(np.float32)
    ahead = np.block([[cos, sin], [-sin, cos]]).astype(ml_dtypes.bfloat16)
    back = np.block([[cos, -sin], [sin, cos]]).astype(ml_dtypes.bfloat16)
    return ahead, back


def slot_kernel(
    scale, at_ref, piece_ref, probe_ref, amp_ref, ahead_ref, back_ref,
    grad_ref, mode_ref, win, far, stacked, middle,
):
    modes, n = probe_ref.shape[1], probe_ref.shape[2]
    wide = n // 2
    row_at, col_at = at_ref[0], at_ref[1]
    row_back = lax.rem(n - row_at, n)
    col_back = lax.rem(n - col_at, n)
    for part in range(2):
        win[part] = pltpu.roll(pltpu.roll(piece_ref[part], row_back, 0), col_back, 1)

    def products(m, left_ref, right_ref):
        for half in range(2):
            for j in range(2):
                cols = slice(j * wide, (j + 1) * wide)
                middle[:, half * n + j * wide : half * n + (j + 1) * wide] = jnp.dot(
                    left_ref[half * n : (half + 1) * n, :],
                    stacked[:, cols],
                    preferred_element_type=jnp.float32,
                ).astype(jnp.bfloat16)
        for half in range(2):
            for j in range(2):
                far[m, half, :, j * wide : (j + 1) * wide] = jnp.dot(
                    middle[...],
                    right_ref[:, half * n + j * wide : half * n + (j + 1) * wide],
                    preferred_element_type=jnp.float32,
                )

    def rows_of(k):
        return pl.ds(pl.multiple_of(k * ROWS, ROWS), ROWS)

    def lower_of(k):
        return pl.ds(pl.multiple_of(n + k * ROWS, ROWS), ROWS)

    @pl.loop(0, modes)
    def _(m):
        @pl.loop(0, n // ROWS)
        def _(k):
            rows = rows_of(k)
            pr, pi = probe_ref[0, m, rows, :], probe_ref[1, m, rows, :]
            wr, wi = win[0, rows, :], win[1, rows, :]
            stacked[rows, :] = (pr * wr - pi * wi).astype(jnp.bfloat16)
            stacked[lower_of(k), :] = (pr * wi + pi * wr).astype(jnp.bfloat16)

        products(m, ahead_ref, back_ref)

    @pl.loop(0, n // ROWS)
    def _(k):
        rows = rows_of(k)
        total = jnp.zeros((ROWS, n), jnp.float32)
        for m in range(modes):
            total += far[m, 0, rows, :] * far[m, 0, rows, :] + far[m, 1, rows, :] * far[m, 1, rows, :]
        factor = amp_ref[rows, :] * lax.rsqrt(jnp.maximum(total, 1.0)) - 1.0
        for m in range(modes):
            far[m, 0, rows, :] = far[m, 0, rows, :] * factor
            far[m, 1, rows, :] = far[m, 1, rows, :] * factor

    @pl.loop(0, modes)
    def _(m):
        @pl.loop(0, n // ROWS)
        def _(k):
            stacked[rows_of(k), :] = far[m, 0, rows_of(k), :].astype(jnp.bfloat16)
            stacked[lower_of(k), :] = far[m, 1, rows_of(k), :].astype(jnp.bfloat16)

        products(m, back_ref, ahead_ref)

    @pl.loop(0, n // ROWS)
    def _(k):
        rows = rows_of(k)
        wr, wi = win[0, rows, :] * scale, win[1, rows, :] * scale
        grad_re = jnp.zeros((ROWS, n), jnp.float32)
        grad_im = jnp.zeros((ROWS, n), jnp.float32)
        for m in range(modes):
            br, bi = far[m, 0, rows, :], far[m, 1, rows, :]
            pr, pi = probe_ref[0, m, rows, :], probe_ref[1, m, rows, :]
            mode_ref[0, m, rows, :] = wr * br + wi * bi
            mode_ref[1, m, rows, :] = wr * bi - wi * br
            grad_re += pr * br + pi * bi
            grad_im += pr * bi - pi * br
        win[0, rows, :] = grad_re
        win[1, rows, :] = grad_im

    for part in range(2):
        grad_ref[part] = pltpu.roll(pltpu.roll(win[part], row_at, 0), col_at, 1)


def slot_terms(at, piece, probe_modes, measured, scale):
    modes, n = probe_modes.shape[1], probe_modes.shape[2]
    ahead, back = block_tables(n)
    vmem = pl.BlockSpec(memory_space=pltpu.VMEM)
    return pl.pallas_call(
        functools.partial(slot_kernel, scale),
        out_shape=(
            jax.ShapeDtypeStruct((2, n, n), jnp.float32),
            jax.ShapeDtypeStruct((2, modes, n, n), jnp.float32),
        ),
        in_specs=[pl.BlockSpec(memory_space=pltpu.SMEM)] + [vmem] * 5,
        out_specs=(vmem, vmem),
        scratch_shapes=[
            pltpu.VMEM((2, n, n), jnp.float32),
            pltpu.VMEM((modes, 2, n, n), jnp.float32),
            pltpu.VMEM((2 * n, n), jnp.bfloat16),
            pltpu.VMEM((n, 2 * n), jnp.bfloat16),
        ],
        compiler_params=pltpu.CompilerParams(vmem_limit_bytes=50 * 2**20),
        cost_estimate=pl.CostEstimate(
            flops=modes * 32 * n**3, bytes_accessed=24 * 2**20, transcendentals=n * n
        ),
    )(at, piece, probe_modes, measured, jnp.asarray(ahead), jnp.asarray(back))


def summed(value, bits):
    if not bits:
        return value
    axis, bit = bits[0]
    upper = (lax.axis_index(axis) >> bit) & 1 == 1
    half = value.shape[0] // 2
    first, second = value[:half], value[half:]
    got = flipped(jnp.where(upper, first, second), axis, bit)
    kept = jnp.where(upper, second, first) + got
    rest = bits[1:]
    if len(bits) == SPLIT_AT[0]:
        quarter = half // 2
        swapped = [rest[1], rest[0]] + rest[2:]
        done = jnp.concatenate([summed(kept[:quarter], rest), summed(kept[quarter:], swapped)])
    else:
        done = summed(kept, rest)
    other = flipped(done, axis, bit)
    return jnp.concatenate([jnp.where(upper, other, done), jnp.where(upper, done, other)])


SPLIT_AT = [0]


def sum_all(value):
    tx_bits = lax.axis_size("tx").bit_length() - 1
    ty_bits = lax.axis_size("ty").bit_length() - 1
    bits = [("tx", bit) for bit in range(tx_bits)] + [("ty", bit) for bit in reversed(range(ty_bits))]
    SPLIT_AT[0] = len(bits)
    flat = value.reshape(-1, value.shape[-1])
    return summed(flat, bits).reshape(value.shape)


def local(specimen, probe_modes, amplitude, offsets, live_slots):
    width = probe_modes.shape[2]
    slots = live_slots.shape[0]
    n_tx = lax.axis_size("tx")
    devices_all = lax.axis_size("ty") * n_tx
    size = width // CHUNKS
    col = lax.axis_index("tx").astype(jnp.int32)
    mate = col ^ 1
    even_at = range(0, n_tx - 2, 2)

    lower = [
        shifted(specimen[:, k * size : (k + 1) * size, :], "ty", -1) for k in range(CHUNKS)
    ]
    meta = jnp.concatenate([offsets.reshape(-1), jnp.sum(live_slots).reshape(1)])
    mate_meta = flipped(meta, "tx", 0)

    def item(held, held_col, others, others_col):
        own = held[4] >= 1
        return jnp.stack([
            jnp.where(own, held[0], others[2]),
            jnp.where(own, held[1], others[3]),
            jnp.where(own, held_col, others_col),
        ])

    mine = item(meta, col, mate_meta, mate)
    theirs = item(mate_meta, mate, meta, col)
    before = lax.ppermute(jnp.stack([mine, theirs]), "tx", [(at, at + 2) for at in even_at])
    measured = jnp.where(meta[4] >= 1, amplitude[0], flipped(amplitude[1], "tx", 0))

    p_at = lax.broadcasted_iota(jnp.int32, (1, 1, width), 2)

    def q_at(k):
        return lax.broadcasted_iota(jnp.int32, (1, size, 1), 1) + k * size

    def picked(k, work):
        q = q_at(k)
        upper_rows = specimen[:, k * size : (k + 1) * size, :]
        lower_rows = specimen[:, width + k * size : width + (k + 1) * size, :]
        own_rows = jnp.where(q >= work[0], upper_rows, lower_rows)
        return jnp.where(q + width < work[0], lower[k], own_rows)

    pieces = []
    for k in range(CHUNKS):
        next_even = lax.ppermute(picked(k, before[0]), "tx", [(at + 2, at) for at in even_at])
        next_odd = lax.ppermute(picked(k, before[1]), "tx", [(at + 2, at + 1) for at in even_at])
        from_next = next_even + next_odd
        from_mate = flipped(picked(k, theirs), "tx", 0)
        own = picked(k, mine)

        def strip(tile):
            return jnp.where(tile == col, own, jnp.where(tile == mate, from_mate, from_next))

        pieces.append(jnp.where(p_at >= mine[1], strip(mine[2]), strip(mine[2] + 1)))
    piece = jnp.concatenate(pieces, axis=1)

    at = jnp.stack([lax.rem(mine[0], width), lax.rem(mine[1], width)])
    scale = 1.0 / math.sqrt(slots * devices_all)
    grad, mode_terms = slot_terms(at, piece, probe_modes, measured, scale)

    def col_mask(work):
        return ((work[2] == col) & (p_at >= work[1])) | ((work[2] + 1 == col) & (p_at < work[1]))

    works = [mine, theirs, before[0], before[1]]
    masks = [col_mask(work) for work in works]
    tops, bottoms, aboves = [], [], []
    for k in range(CHUNKS):
        q = q_at(k)
        mine_k = grad[:, k * size : (k + 1) * size, :]
        terms = [
            mine_k,
            flipped(mine_k, "tx", 0),
            lax.ppermute(mine_k, "tx", [(at, at + 2) for at in even_at]),
            lax.ppermute(mine_k, "tx", [(at + 1, at + 2) for at in even_at]),
        ]
        top = bottom = beyond = jnp.zeros((), jnp.float32)
        for term, work, mask in zip(terms, works, masks):
            row = work[0]
            top += jnp.where(mask & (q >= row), term, 0.0)
            bottom += jnp.where(mask & (q < row) & (q + width >= row), term, 0.0)
            beyond += jnp.where(mask & (q + width < row), term, 0.0)
        aboves.append(shifted(beyond, "ty", 1))
        tops.append(top)
        bottoms.append(bottom)
    probe_grad = sum_all(mode_terms)
    tops = [top + above for top, above in zip(tops, aboves)]
    return (jnp.concatenate(tops + bottoms, axis=1), probe_grad)


def solution(mesh):
    return jax.shard_map(
        local,
        mesh=mesh,
        in_specs=(
            P(None, "ty", "tx"),
            P(),
            P(("ty", "tx"), None, None),
            P(("ty", "tx"), None),
            P(("ty", "tx")),
        ),
        out_specs=(P(None, "ty", "tx"), P()),
        check_vma=False,
    )
```

```python
import functools
import math

import jax
import jax.numpy as jnp
import ml_dtypes
import numpy as np
from jax import lax
from jax.experimental import pallas as pl
from jax.experimental.pallas import tpu as pltpu
from jax.sharding import PartitionSpec as P

CHUNKS = 2
ROWS = 32


def flipped(value, axis, bit):
    mask = 1 << bit
    return lax.ppermute(value, axis, [(at, at ^ mask) for at in range(lax.axis_size(axis))])


def shifted(value, axis, steps):
    count = lax.axis_size(axis)
    first, last = max(0, -steps), min(count, count - steps)
    return lax.ppermute(value, axis, [(at, at + steps) for at in range(first, last)])


def block_tables(length):
    index = np.arange(length)
    angle = (index[:, None] * index[None, :] % length) * (2.0 * math.pi / length)
    scale = 1.0 / math.sqrt(length)
    cos = (np.cos(angle) * scale).astype(np.float32)
    sin = (np.sin(angle) * scale).astype(np.float32)
    ahead = np.block([[cos, sin], [-sin, cos]]).astype(ml_dtypes.bfloat16)
    back = np.block([[cos, -sin], [sin, cos]]).astype(ml_dtypes.bfloat16)
    return ahead, back


def slot_kernel(
    scale, at_ref, piece_ref, probe_ref, amp_ref, ahead_ref, back_ref,
    grad_ref, mode_ref, win, far, stacked, middle,
):
    modes, n = probe_ref.shape[1], probe_ref.shape[2]
    wide = n // 2
    row_at, col_at = at_ref[0], at_ref[1]
    row_back = lax.rem(n - row_at, n)
    col_back = lax.rem(n - col_at, n)
    for part in range(2):
        win[part] = pltpu.roll(pltpu.roll(piece_ref[part], row_back, 0), col_back, 1)

    def products(m, left_ref, right_ref):
        for half in range(2):
            for j in range(2):
                cols = slice(j * wide, (j + 1) * wide)
                middle[:, half * n + j * wide : half * n + (j + 1) * wide] = jnp.dot(
                    left_ref[half * n : (half + 1) * n, :],
                    stacked[:, cols],
                    preferred_element_type=jnp.float32,
                ).astype(jnp.bfloat16)
        for half in range(2):
            for j in range(2):
                far[m, half, :, j * wide : (j + 1) * wide] = jnp.dot(
                    middle[...],
                    right_ref[:, half * n + j * wide : half * n + (j + 1) * wide],
                    preferred_element_type=jnp.float32,
                )

    def rows_of(k):
        return pl.ds(pl.multiple_of(k * ROWS, ROWS), ROWS)

    def lower_of(k):
        return pl.ds(pl.multiple_of(n + k * ROWS, ROWS), ROWS)

    @pl.loop(0, modes)
    def _(m):
        @pl.loop(0, n // ROWS)
        def _(k):
            rows = rows_of(k)
            pr, pi = probe_ref[0, m, rows, :], probe_ref[1, m, rows, :]
            wr, wi = win[0, rows, :], win[1, rows, :]
            stacked[rows, :] = (pr * wr - pi * wi).astype(jnp.bfloat16)
            stacked[lower_of(k), :] = (pr * wi + pi * wr).astype(jnp.bfloat16)

        products(m, ahead_ref, back_ref)

    @pl.loop(0, n // ROWS)
    def _(k):
        rows = rows_of(k)
        total = jnp.zeros((ROWS, n), jnp.float32)
        for m in range(modes):
            total += far[m, 0, rows, :] * far[m, 0, rows, :] + far[m, 1, rows, :] * far[m, 1, rows, :]
        factor = amp_ref[rows, :] * lax.rsqrt(jnp.maximum(total, 1.0)) - 1.0
        for m in range(modes):
            far[m, 0, rows, :] = far[m, 0, rows, :] * factor
            far[m, 1, rows, :] = far[m, 1, rows, :] * factor

    @pl.loop(0, modes)
    def _(m):
        @pl.loop(0, n // ROWS)
        def _(k):
            stacked[rows_of(k), :] = far[m, 0, rows_of(k), :].astype(jnp.bfloat16)
            stacked[lower_of(k), :] = far[m, 1, rows_of(k), :].astype(jnp.bfloat16)

        products(m, back_ref, ahead_ref)

    @pl.loop(0, n // ROWS)
    def _(k):
        rows = rows_of(k)
        wr, wi = win[0, rows, :] * scale, win[1, rows, :] * scale
        grad_re = jnp.zeros((ROWS, n), jnp.float32)
        grad_im = jnp.zeros((ROWS, n), jnp.float32)
        for m in range(modes):
            br, bi = far[m, 0, rows, :], far[m, 1, rows, :]
            pr, pi = probe_ref[0, m, rows, :], probe_ref[1, m, rows, :]
            mode_ref[0, m, rows, :] = wr * br + wi * bi
            mode_ref[1, m, rows, :] = wr * bi - wi * br
            grad_re += pr * br + pi * bi
            grad_im += pr * bi - pi * br
        win[0, rows, :] = grad_re
        win[1, rows, :] = grad_im

    for part in range(2):
        grad_ref[part] = pltpu.roll(pltpu.roll(win[part], row_at, 0), col_at, 1)


def slot_terms(at, piece, probe_modes, measured, scale):
    modes, n = probe_modes.shape[1], probe_modes.shape[2]
    ahead, back = block_tables(n)
    vmem = pl.BlockSpec(memory_space=pltpu.VMEM)
    return pl.pallas_call(
        functools.partial(slot_kernel, scale),
        out_shape=(
            jax.ShapeDtypeStruct((2, n, n), jnp.float32),
            jax.ShapeDtypeStruct((2, modes, n, n), jnp.float32),
        ),
        in_specs=[pl.BlockSpec(memory_space=pltpu.SMEM)] + [vmem] * 5,
        out_specs=(vmem, vmem),
        scratch_shapes=[
            pltpu.VMEM((2, n, n), jnp.float32),
            pltpu.VMEM((modes, 2, n, n), jnp.float32),
            pltpu.VMEM((2 * n, n), jnp.bfloat16),
            pltpu.VMEM((n, 2 * n), jnp.bfloat16),
        ],
        compiler_params=pltpu.CompilerParams(vmem_limit_bytes=50 * 2**20),
        cost_estimate=pl.CostEstimate(
            flops=modes * 32 * n**3, bytes_accessed=24 * 2**20, transcendentals=n * n
        ),
    )(at, piece, probe_modes, measured, jnp.asarray(ahead), jnp.asarray(back))


def token(*values):
    bad = jnp.zeros((), jnp.bool_)
    for value in values:
        bad |= jnp.isnan(value[(0,) * value.ndim])
    return bad.astype(jnp.int32)


def halved(value, axis, bit, after=0):
    upper = ((lax.axis_index(axis) + after) >> bit) & 1 == 1
    half = value.shape[0] // 2
    first, second = value[:half], value[half:]
    got = flipped(jnp.where(upper, first, second), axis, bit)
    return jnp.where(upper, second, first) + got


def doubled(value, axis, bit, after=0):
    upper = ((lax.axis_index(axis) + after) >> bit) & 1 == 1
    other = flipped(value, axis, bit)
    return jnp.concatenate([jnp.where(upper, other, value), jnp.where(upper, value, other)])


def summed_inner(value, bits):
    for axis, bit in bits:
        value = halved(value, axis, bit)
    for axis, bit in reversed(bits):
        value = doubled(value, axis, bit)
    return value


def local(specimen, probe_modes, amplitude, offsets, live_slots):
    width = probe_modes.shape[2]
    slots = live_slots.shape[0]
    n_tx = lax.axis_size("tx")
    devices_all = lax.axis_size("ty") * n_tx
    size = width // CHUNKS
    col = lax.axis_index("tx").astype(jnp.int32)
    mate = col ^ 1
    even_at = range(0, n_tx - 2, 2)

    lower = [
        shifted(specimen[:, k * size : (k + 1) * size, :], "ty", -1) for k in range(CHUNKS)
    ]
    meta = jnp.concatenate([offsets.reshape(-1), jnp.sum(live_slots).reshape(1)])
    mate_meta = flipped(meta, "tx", 0)

    def item(held, held_col, others, others_col):
        own = held[4] >= 1
        return jnp.stack([
            jnp.where(own, held[0], others[2]),
            jnp.where(own, held[1], others[3]),
            jnp.where(own, held_col, others_col),
        ])

    mine = item(meta, col, mate_meta, mate)
    theirs = item(mate_meta, mate, meta, col)
    before = lax.ppermute(jnp.stack([mine, theirs]), "tx", [(at, at + 2) for at in even_at])
    measured = jnp.where(meta[4] >= 1, amplitude[0], flipped(amplitude[1], "tx", 0))

    p_at = lax.broadcasted_iota(jnp.int32, (1, 1, width), 2)

    def q_at(k):
        return lax.broadcasted_iota(jnp.int32, (1, size, 1), 1) + k * size

    def picked(k, work):
        q = q_at(k)
        upper_rows = specimen[:, k * size : (k + 1) * size, :]
        lower_rows = specimen[:, width + k * size : width + (k + 1) * size, :]
        own_rows = jnp.where(q >= work[0], upper_rows, lower_rows)
        return jnp.where(q + width < work[0], lower[k], own_rows)

    pieces = []
    for k in range(CHUNKS):
        next_even = lax.ppermute(picked(k, before[0]), "tx", [(at + 2, at) for at in even_at])
        next_odd = lax.ppermute(picked(k, before[1]), "tx", [(at + 2, at + 1) for at in even_at])
        from_next = next_even + next_odd
        from_mate = flipped(picked(k, theirs), "tx", 0)
        own = picked(k, mine)

        def strip(tile):
            return jnp.where(tile == col, own, jnp.where(tile == mate, from_mate, from_next))

        pieces.append(jnp.where(p_at >= mine[1], strip(mine[2]), strip(mine[2] + 1)))
    piece = jnp.concatenate(pieces, axis=1)

    at = jnp.stack([lax.rem(mine[0], width), lax.rem(mine[1], width)])
    scale = 1.0 / math.sqrt(slots * devices_all)
    grad, mode_terms = slot_terms(at, piece, probe_modes, measured, scale)

    def col_mask(work):
        return ((work[2] == col) & (p_at >= work[1])) | ((work[2] + 1 == col) & (p_at < work[1]))

    works = [mine, theirs, before[0], before[1]]
    masks = [col_mask(work) for work in works]
    terms = []
    for k in range(CHUNKS):
        mine_k = grad[:, k * size : (k + 1) * size, :]
        terms.append([
            mine_k,
            flipped(mine_k, "tx", 0),
            lax.ppermute(mine_k, "tx", [(at, at + 2) for at in even_at]),
            lax.ppermute(mine_k, "tx", [(at + 1, at + 2) for at in even_at]),
        ])

    def placed(k, keep, after=0):
        total = jnp.zeros((), jnp.float32)
        for term, work, mask in zip(terms[k], works, masks):
            total += jnp.where(mask & keep(q_at(k), work[0] + after), term, 0.0)
        return total

    def beyond(q, row):
        return q + width < row

    bits = [("tx", bit) for bit in range(1, n_tx.bit_length() - 1)]
    swapped = [bits[1], bits[0]] + bits[2:]
    deep = [("ty", bit) for bit in reversed(range(lax.axis_size("ty").bit_length() - 1))]
    flat = mode_terms.reshape(-1, width)
    kept = halved(flat, "tx", 0)
    quarter = kept.shape[0] // 2
    first_after = token(*terms[0][1:])
    above_first = shifted(placed(0, beyond), "ty", 1)
    sums = [
        halved(part, *order[0], first_after)
        for part, order in ((kept[:quarter], bits), (kept[quarter:], swapped))
    ]
    second_after = token(*terms[1][1:])
    above_second = shifted(placed(1, beyond), "ty", 1)
    sums = [
        halved(part, *order[1], token(above_first) + second_after)
        for part, order in zip(sums, (bits, swapped))
    ]
    sums = [summed_inner(part, order[2:] + deep) for part, order in zip(sums, (bits, swapped))]
    last_after = token(above_second)
    for at_bit in (1, 0):
        sums = [
            doubled(part, *order[at_bit], last_after) for part, order in zip(sums, (bits, swapped))
        ]
    probe_grad = doubled(jnp.concatenate(sums), "tx", 0).reshape(mode_terms.shape)
    aboves = [above_first, above_second]
    tops = [placed(k, lambda q, row: q >= row) + aboves[k] for k in range(CHUNKS)]
    bottoms = [placed(k, lambda q, row: (q < row) & (q + width >= row)) for k in range(CHUNKS)]
    return (jnp.concatenate(tops + bottoms, axis=1), probe_grad)


def solution(mesh):
    return jax.shard_map(
        local,
        mesh=mesh,
        in_specs=(
            P(None, "ty", "tx"),
            P(),
            P(("ty", "tx"), None, None),
            P(("ty", "tx"), None),
            P(("ty", "tx")),
        ),
        out_specs=(P(None, "ty", "tx"), P()),
        check_vma=False,
    )
```

```python
import functools
import math

import jax
import jax.numpy as jnp
import ml_dtypes
import numpy as np
from jax import lax
from jax.experimental import pallas as pl
from jax.experimental.pallas import tpu as pltpu
from jax.sharding import PartitionSpec as P

CHUNKS = 1
ROWS = 32


def flipped(value, axis, bit):
    mask = 1 << bit
    return lax.ppermute(value, axis, [(at, at ^ mask) for at in range(lax.axis_size(axis))])


def shifted(value, axis, steps):
    count = lax.axis_size(axis)
    first, last = max(0, -steps), min(count, count - steps)
    return lax.ppermute(value, axis, [(at, at + steps) for at in range(first, last)])


def block_tables(length):
    index = np.arange(length)
    angle = (index[:, None] * index[None, :] % length) * (2.0 * math.pi / length)
    scale = 1.0 / math.sqrt(length)
    cos = (np.cos(angle) * scale).astype(np.float32)
    sin = (np.sin(angle) * scale).astype(np.float32)
    ahead = np.block([[cos, sin], [-sin, cos]]).astype(ml_dtypes.bfloat16)
    back = np.block([[cos, -sin], [sin, cos]]).astype(ml_dtypes.bfloat16)
    return ahead, back


def slot_kernel(
    scale, at_ref, piece_ref, probe_ref, amp_ref, ahead_ref, back_ref,
    grad_ref, mode_ref, win, far, stacked, middle,
):
    modes, n = probe_ref.shape[1], probe_ref.shape[2]
    wide = n // 2
    row_at, col_at = at_ref[0], at_ref[1]
    row_back = lax.rem(n - row_at, n)
    col_back = lax.rem(n - col_at, n)
    for part in range(2):
        win[part] = pltpu.roll(pltpu.roll(piece_ref[part], row_back, 0), col_back, 1)

    def products(m, left_ref, right_ref):
        for half in range(2):
            for j in range(2):
                cols = slice(j * wide, (j + 1) * wide)
                middle[:, half * n + j * wide : half * n + (j + 1) * wide] = jnp.dot(
                    left_ref[half * n : (half + 1) * n, :],
                    stacked[:, cols],
                    preferred_element_type=jnp.float32,
                ).astype(jnp.bfloat16)
        for half in range(2):
            for j in range(2):
                far[m, half, :, j * wide : (j + 1) * wide] = jnp.dot(
                    middle[...],
                    right_ref[:, half * n + j * wide : half * n + (j + 1) * wide],
                    preferred_element_type=jnp.float32,
                )

    def rows_of(k):
        return pl.ds(pl.multiple_of(k * ROWS, ROWS), ROWS)

    def lower_of(k):
        return pl.ds(pl.multiple_of(n + k * ROWS, ROWS), ROWS)

    @pl.loop(0, modes)
    def _(m):
        @pl.loop(0, n // ROWS)
        def _(k):
            rows = rows_of(k)
            pr, pi = probe_ref[0, m, rows, :], probe_ref[1, m, rows, :]
            wr, wi = win[0, rows, :], win[1, rows, :]
            stacked[rows, :] = (pr * wr - pi * wi).astype(jnp.bfloat16)
            stacked[lower_of(k), :] = (pr * wi + pi * wr).astype(jnp.bfloat16)

        products(m, ahead_ref, back_ref)

    @pl.loop(0, n // ROWS)
    def _(k):
        rows = rows_of(k)
        total = jnp.zeros((ROWS, n), jnp.float32)
        for m in range(modes):
            total += far[m, 0, rows, :] * far[m, 0, rows, :] + far[m, 1, rows, :] * far[m, 1, rows, :]
        factor = amp_ref[rows, :] * lax.rsqrt(jnp.maximum(total, 1.0)) - 1.0
        for m in range(modes):
            far[m, 0, rows, :] = far[m, 0, rows, :] * factor
            far[m, 1, rows, :] = far[m, 1, rows, :] * factor

    @pl.loop(0, modes)
    def _(m):
        @pl.loop(0, n // ROWS)
        def _(k):
            stacked[rows_of(k), :] = far[m, 0, rows_of(k), :].astype(jnp.bfloat16)
            stacked[lower_of(k), :] = far[m, 1, rows_of(k), :].astype(jnp.bfloat16)

        products(m, back_ref, ahead_ref)

    @pl.loop(0, n // ROWS)
    def _(k):
        rows = rows_of(k)
        wr, wi = win[0, rows, :] * scale, win[1, rows, :] * scale
        grad_re = jnp.zeros((ROWS, n), jnp.float32)
        grad_im = jnp.zeros((ROWS, n), jnp.float32)
        for m in range(modes):
            br, bi = far[m, 0, rows, :], far[m, 1, rows, :]
            pr, pi = probe_ref[0, m, rows, :], probe_ref[1, m, rows, :]
            mode_ref[0, m, rows, :] = wr * br + wi * bi
            mode_ref[1, m, rows, :] = wr * bi - wi * br
            grad_re += pr * br + pi * bi
            grad_im += pr * bi - pi * br
        win[0, rows, :] = grad_re
        win[1, rows, :] = grad_im

    for part in range(2):
        grad_ref[part] = pltpu.roll(pltpu.roll(win[part], row_at, 0), col_at, 1)


def slot_terms(at, piece, probe_modes, measured, scale):
    modes, n = probe_modes.shape[1], probe_modes.shape[2]
    ahead, back = block_tables(n)
    vmem = pl.BlockSpec(memory_space=pltpu.VMEM)
    return pl.pallas_call(
        functools.partial(slot_kernel, scale),
        out_shape=(
            jax.ShapeDtypeStruct((2, n, n), jnp.float32),
            jax.ShapeDtypeStruct((2, modes, n, n), jnp.float32),
        ),
        in_specs=[pl.BlockSpec(memory_space=pltpu.SMEM)] + [vmem] * 5,
        out_specs=(vmem, vmem),
        scratch_shapes=[
            pltpu.VMEM((2, n, n), jnp.float32),
            pltpu.VMEM((modes, 2, n, n), jnp.float32),
            pltpu.VMEM((2 * n, n), jnp.bfloat16),
            pltpu.VMEM((n, 2 * n), jnp.bfloat16),
        ],
        compiler_params=pltpu.CompilerParams(vmem_limit_bytes=50 * 2**20),
        cost_estimate=pl.CostEstimate(
            flops=modes * 32 * n**3, bytes_accessed=24 * 2**20, transcendentals=n * n
        ),
    )(at, piece, probe_modes, measured, jnp.asarray(ahead), jnp.asarray(back))


def token(*values):
    bad = jnp.zeros((), jnp.bool_)
    for value in values:
        bad |= jnp.isnan(value[(0,) * value.ndim])
    return bad.astype(jnp.int32)


def halved(value, axis, bit, after=0):
    upper = ((lax.axis_index(axis) + after) >> bit) & 1 == 1
    half = value.shape[0] // 2
    first, second = value[:half], value[half:]
    got = flipped(jnp.where(upper, first, second), axis, bit)
    return jnp.where(upper, second, first) + got


def doubled(value, axis, bit, after=0):
    upper = ((lax.axis_index(axis) + after) >> bit) & 1 == 1
    other = flipped(value, axis, bit)
    return jnp.concatenate([jnp.where(upper, other, value), jnp.where(upper, value, other)])


def summed_inner(value, bits):
    for axis, bit in bits:
        value = halved(value, axis, bit)
    for axis, bit in reversed(bits):
        value = doubled(value, axis, bit)
    return value


def local(specimen, probe_modes, amplitude, offsets, live_slots):
    width = probe_modes.shape[2]
    slots = live_slots.shape[0]
    n_tx = lax.axis_size("tx")
    devices_all = lax.axis_size("ty") * n_tx
    size = width // CHUNKS
    col = lax.axis_index("tx").astype(jnp.int32)
    mate = col ^ 1
    even_at = range(0, n_tx - 2, 2)

    lower = [
        shifted(specimen[:, k * size : (k + 1) * size, :], "ty", -1) for k in range(CHUNKS)
    ]
    meta = jnp.concatenate([offsets.reshape(-1), jnp.sum(live_slots).reshape(1)])
    mate_meta = flipped(meta, "tx", 0)

    def item(held, held_col, others, others_col):
        own = held[4] >= 1
        return jnp.stack([
            jnp.where(own, held[0], others[2]),
            jnp.where(own, held[1], others[3]),
            jnp.where(own, held_col, others_col),
        ])

    mine = item(meta, col, mate_meta, mate)
    theirs = item(mate_meta, mate, meta, col)
    before = lax.ppermute(jnp.stack([mine, theirs]), "tx", [(at, at + 2) for at in even_at])
    measured = jnp.where(meta[4] >= 1, amplitude[0], flipped(amplitude[1], "tx", 0))

    p_at = lax.broadcasted_iota(jnp.int32, (1, 1, width), 2)

    def q_at(k):
        return lax.broadcasted_iota(jnp.int32, (1, size, 1), 1) + k * size

    def picked(k, work):
        q = q_at(k)
        upper_rows = specimen[:, k * size : (k + 1) * size, :]
        lower_rows = specimen[:, width + k * size : width + (k + 1) * size, :]
        own_rows = jnp.where(q >= work[0], upper_rows, lower_rows)
        return jnp.where(q + width < work[0], lower[k], own_rows)

    pieces = []
    for k in range(CHUNKS):
        next_even = lax.ppermute(picked(k, before[0]), "tx", [(at + 2, at) for at in even_at])
        next_odd = lax.ppermute(picked(k, before[1]), "tx", [(at + 2, at + 1) for at in even_at])
        from_next = next_even + next_odd
        from_mate = flipped(picked(k, theirs), "tx", 0)
        own = picked(k, mine)

        def strip(tile):
            return jnp.where(tile == col, own, jnp.where(tile == mate, from_mate, from_next))

        pieces.append(jnp.where(p_at >= mine[1], strip(mine[2]), strip(mine[2] + 1)))
    piece = jnp.concatenate(pieces, axis=1)

    at = jnp.stack([lax.rem(mine[0], width), lax.rem(mine[1], width)])
    scale = 1.0 / math.sqrt(slots * devices_all)
    grad, mode_terms = slot_terms(at, piece, probe_modes, measured, scale)

    def col_mask(work):
        return ((work[2] == col) & (p_at >= work[1])) | ((work[2] + 1 == col) & (p_at < work[1]))

    works = [mine, theirs, before[0], before[1]]
    masks = [col_mask(work) for work in works]
    terms = []
    for k in range(CHUNKS):
        mine_k = grad[:, k * size : (k + 1) * size, :]
        terms.append([
            mine_k,
            flipped(mine_k, "tx", 0),
            lax.ppermute(mine_k, "tx", [(at, at + 2) for at in even_at]),
            lax.ppermute(mine_k, "tx", [(at + 1, at + 2) for at in even_at]),
        ])

    def placed(k, keep, after=0):
        total = jnp.zeros((), jnp.float32)
        for term, work, mask in zip(terms[k], works, masks):
            total += jnp.where(mask & keep(q_at(k), work[0] + after), term, 0.0)
        return total

    def beyond(q, row):
        return q + width < row

    bits = [("tx", bit) for bit in range(1, n_tx.bit_length() - 1)]
    swapped = [bits[1], bits[0]] + bits[2:]
    deep = [("ty", bit) for bit in reversed(range(lax.axis_size("ty").bit_length() - 1))]
    flat = mode_terms.reshape(-1, width)
    kept = halved(flat, "tx", 0)
    quarter = kept.shape[0] // 2
    sums = [
        halved(part, *order[0])
        for part, order in ((kept[:quarter], bits), (kept[quarter:], swapped))
    ]
    aside_after = token(*terms[0][1:])
    above = shifted(placed(0, beyond), "ty", 1)
    sums = [
        halved(part, *order[1], aside_after) for part, order in zip(sums, (bits, swapped))
    ]
    sums = [summed_inner(part, order[2:] + deep) for part, order in zip(sums, (bits, swapped))]
    last_after = token(above)
    for at_bit in (1, 0):
        sums = [
            doubled(part, *order[at_bit], last_after) for part, order in zip(sums, (bits, swapped))
        ]
    probe_grad = doubled(jnp.concatenate(sums), "tx", 0).reshape(mode_terms.shape)
    tops = [placed(k, lambda q, row: q >= row) + above for k in range(CHUNKS)]
    bottoms = [placed(k, lambda q, row: (q < row) & (q + width >= row)) for k in range(CHUNKS)]
    return (jnp.concatenate(tops + bottoms, axis=1), probe_grad)


def solution(mesh):
    return jax.shard_map(
        local,
        mesh=mesh,
        in_specs=(
            P(None, "ty", "tx"),
            P(),
            P(("ty", "tx"), None, None),
            P(("ty", "tx"), None),
            P(("ty", "tx")),
        ),
        out_specs=(P(None, "ty", "tx"), P()),
        check_vma=False,
    )
```
